32 devices in a mesh: prow: 4 (over z), pcol: 4 (over y, core), pl: 2 (over x).
Axes of the slice: x: 2, y: 2, z: 4, core: 2. Of those that a mesh axis runs over, the one named last changes fastest.
Arguments:
- factor_cols: bfloat16 [32768, 512], P(('prow', 'pcol'), 'pl'), may hold values from -0.25 to 0.25
- modal_at_loads: bfloat16 [2048, 32768], P(None, ('prow', 'pcol')), may hold values from -0.03125 to 0.03125
- mode_shapes: bfloat16 [8192, 2048], P(('prow', 'pl')), may hold values from -0.125 to 0.125
- natural_freq: float32 [2048], replicated, may hold values from 0.5 to 2
- damping: float32 [2048], replicated, may hold values from 0.05 to 0.2
Outputs:
- cospectrum: float32 [8192, 8192], P(('prow', 'pl'), 'pcol')
The draws below stay inside these ranges and needn't reach their ends.
All inputs are finite; a program needn't handle non-finite values.
Results may differ from the reference program's by a relative error of at most 0.022.
Values may be sent and summed in bfloat16 or wider, within the bound.
No kernel may reach another device: no remote copies, remote signals or barrier semaphores. Data moves between devices by JAX's collectives and lax.ppermute only.
A program may use at most 128 MiB of HBM per device.

```python
import math
import jax
import jax.numpy as jnp

NLOAD = 32768
MODES = 2048
RESP = 8192
PSEUDO = 512


def block_scale(own_key, dims, split, low, high):
    level, own = 1.0, jax.random.fold_in(own_key, 6)
    for axis_at, shards_of in split:
        heights = jnp.exp(jax.random.uniform(jax.random.fold_in(own, axis_at), (shards_of,), jnp.float32, low / len(split), high / len(split)))
        level = level * jnp.repeat(heights, dims[axis_at] // shards_of).reshape([-1 if axis == axis_at else 1 for axis in range(len(dims))])
    return level


def centred(own_key, extent, scale, most, split=(), dtype=jnp.bfloat16):
    level = block_scale(own_key, extent, split, -0.22, 0.18) if split else 1.0
    entries = jax.random.normal(own_key, extent, jnp.float32) * scale * level
    return jnp.minimum(jnp.maximum(entries, -most), most).astype(dtype)


def setup_inputs(seed: int = 0) -> dict:
    streams_of = jax.random.split(jax.random.key(seed), 6)
    return {
        "factor_cols": centred(streams_of[0], (NLOAD, PSEUDO), PSEUDO ** -0.5, 0.25, ((0, 16), (1, 2))),
        "modal_at_loads": centred(streams_of[1], (MODES, NLOAD), NLOAD ** -0.5, 0.03125, ((1, 16),)),
        "mode_shapes": centred(streams_of[2], (RESP, MODES), MODES ** -0.5, 0.125, ((0, 8),)),
        "natural_freq": jnp.clip(jnp.exp(jax.random.uniform(streams_of[3], (MODES,), jnp.float32, math.log(0.5), math.log(2.0))), 0.5, 2.0),
        "damping": jnp.clip(jnp.exp(jax.random.uniform(streams_of[4], (MODES,), jnp.float32, math.log(0.05), math.log(0.2))), 0.05, 0.2),
    }


def transfer_pair(natural_freq, damping):
    detuning = natural_freq * natural_freq - 1.0
    damper = 2.0 * damping * natural_freq
    modulus = detuning * detuning + damper * damper
    return detuning / modulus, -damper / modulus


def reference(factor_cols, modal_at_loads, mode_shapes, natural_freq, damping):
    in_phase, quadrature = transfer_pair(natural_freq, damping)
    modal_load = jnp.dot(modal_at_loads, factor_cols, preferred_element_type=jnp.float32).astype(jnp.bfloat16)
    modal_wide = modal_load.astype(jnp.float32)
    pseudo_real = (in_phase[:, None] * modal_wide).astype(jnp.bfloat16)
    pseudo_imag = (quadrature[:, None] * modal_wide).astype(jnp.bfloat16)
    stacked = jnp.concatenate([pseudo_real, pseudo_imag], axis=1)
    modal_gram = jnp.dot(stacked, stacked.T, preferred_element_type=jnp.float32).astype(jnp.bfloat16)
    weighted = jnp.dot(mode_shapes, modal_gram, preferred_element_type=jnp.float32).astype(jnp.bfloat16)
    return jnp.dot(weighted, mode_shapes.T, preferred_element_type=jnp.float32)
```

```python
import functools

import jax
import jax.numpy as jnp
from jax import lax
from jax.experimental import pallas as pl
from jax.experimental.pallas import tpu as pltpu
from jax.sharding import PartitionSpec as P

AXES = ("prow", "pcol", "pl")
CORES = 2
CHUNKS = 4
LATE = 0
WIDE = 512
VMEM_BYTES = 48 * 1024 * 1024


def transfer_pair(natural_freq, damping):
    detuning = natural_freq * natural_freq - 1.0
    damper = 2.0 * damping * natural_freq
    modulus = detuning * detuning + damper * damper
    return detuning / modulus, -damper / modulus


def moves(sizes, source_of):
    rows, cols, groups = sizes
    pairs = []
    for i in range(rows):
        for j in range(cols):
            for k in range(groups):
                a, b, c = source_of(i, j, k)
                pairs.append(((a * cols + b) * groups + c, (i * cols + j) * groups + k))
    return pairs


def swap(array, sizes, di, dj, dk):
    return lax.ppermute(array, AXES, moves(sizes, lambda i, j, k: (i ^ di, j ^ dj, k ^ dk)))


def across(array, sizes, flip):
    return lax.ppermute(array, AXES, moves(sizes, lambda i, j, k: (j, i ^ flip, k)))


def outer_rows(left_rows, right_rows):
    return lax.dot_general(
        left_rows, right_rows, (((1,), (1,)), ((), ())), preferred_element_type=jnp.float32
    )


def load_kernel(rows, spots, scale, *refs):
    out = refs[-1]
    blocks = refs[: spots.shape[0] - 1]
    for at, block in enumerate(blocks):
        for part in range(block.shape[0] // rows):
            first = pl.multiple_of(spots[1 + at] + (spots[0] ^ part) * rows, rows)
            load = block[part * rows : (part + 1) * rows, :].astype(jnp.float32)
            out[pl.ds(first, rows), :] = (scale[0, pl.ds(first, rows), :] * load).astype(out.dtype)


def place_loads(blocks, firsts, own_row, rows, group, groups, scale, loads):
    modes, wide = scale.shape[1], blocks[0].shape[1]
    spots = jnp.stack([own_row, *firsts]).astype(jnp.int32)
    column = jnp.reshape(group, (1,)).astype(jnp.int32)
    given = [] if loads is None else [loads]
    return pl.pallas_call(
        lambda spots, column, *refs: load_kernel(rows, spots, *refs),
        grid_spec=pltpu.PrefetchScalarGridSpec(
            num_scalar_prefetch=2,
            grid=(2,),
            in_specs=[pl.BlockSpec((1, modes, 1), lambda g, spots, column: (g, 0, 0))]
            + [pl.BlockSpec(b.shape, lambda g, spots, column: (0, 0)) for b in blocks]
            + [pl.BlockSpec(memory_space=pl.ANY) for _ in given],
            out_specs=pl.BlockSpec((modes, wide), lambda g, spots, column: (0, g * groups + column[0])),
        ),
        out_shape=jax.ShapeDtypeStruct((modes, 2 * groups * wide), jnp.bfloat16),
        input_output_aliases={3 + len(blocks): 0} if given else {},
        compiler_params=pltpu.CompilerParams(vmem_limit_bytes=VMEM_BYTES),
    )(spots, column, scale, *blocks, *given)


def shape_kernel(place, shapes, loads, left, *refs):
    out = refs[-1]
    right = jnp.dot(shapes[...], loads[...], preferred_element_type=jnp.float32).astype(jnp.bfloat16)
    part = outer_rows(left[...], right)

    @pl.when(pl.program_id(0) == 0)
    def _():
        out[...] = part

    @pl.when(pl.program_id(0) != 0)
    def _():
        out[...] += part


def place_panel(shapes, loads, left, place, columns, panel):
    modes, wide = loads.shape
    rows, chunk = left.shape[0], shapes.shape[0]
    step = min(WIDE, wide)
    given = [] if panel is None else [panel]
    return pl.pallas_call(
        shape_kernel,
        grid_spec=pltpu.PrefetchScalarGridSpec(
            num_scalar_prefetch=1,
            grid=(wide // step,),
            in_specs=[
                pl.BlockSpec((chunk, modes), lambda g, place: (0, 0)),
                pl.BlockSpec((modes, step), lambda g, place: (0, g)),
                pl.BlockSpec((rows, step), lambda g, place: (0, g)),
            ]
            + [pl.BlockSpec(memory_space=pl.ANY) for _ in given],
            out_specs=pl.BlockSpec((rows, chunk), lambda g, place: (0, place[0])),
        ),
        out_shape=jax.ShapeDtypeStruct((rows, columns), jnp.float32),
        input_output_aliases={4: 0} if given else {},
        compiler_params=pltpu.CompilerParams(vmem_limit_bytes=VMEM_BYTES),
        cost_estimate=pl.CostEstimate(
            flops=2 * chunk * wide * (modes + rows),
            bytes_accessed=2 * wide * (modes + rows) + 2 * chunk * modes + 4 * rows * chunk,
            transcendentals=0,
        ),
    )(jnp.reshape(place, (1,)).astype(jnp.int32), shapes, loads, left, *given)


def body(sizes, factor_cols, modal_at_loads, mode_shapes, natural_freq, damping):
    n_rows, n_cols, n_groups = sizes
    n_high = n_cols // CORES
    row, col, group = (lax.axis_index(axis) for axis in AXES)
    high, core = col // CORES, col % CORES
    scale = jnp.stack(transfer_pair(natural_freq, damping))[:, :, None]

    own_rows = mode_shapes.shape[0]
    chunk = max(own_rows // CHUNKS, min(own_rows, 128))
    chunks = own_rows // chunk
    same = [
        across(mode_shapes[q * chunk : (q + 1) * chunk], sizes, CORES * (q % 2)) for q in range(chunks)
    ]
    other = [[swap(piece, sizes, 0, 0, d) for d in range(1, n_groups)] for piece in same]

    modes = modal_at_loads.shape[0]
    half, block = modes // CORES, modes // (n_rows * n_cols)
    away = lax.dynamic_slice_in_dim(modal_at_loads, (1 - core) * half, half, 0)
    here = lax.dynamic_slice_in_dim(modal_at_loads, core * half, half, 0)
    sent = jnp.dot(away, factor_cols, preferred_element_type=jnp.float32).astype(jnp.bfloat16)
    came = swap(sent, sizes, 0, 1, 0)
    partial = jnp.dot(here, factor_cols, preferred_element_type=jnp.float32) + came.astype(jnp.float32)
    partial = partial.astype(jnp.bfloat16)
    total = None
    for dh in range(n_high):
        for dr in range(n_rows):
            first = ((high ^ dh) * n_rows + (row ^ dr)) * block
            part = lax.dynamic_slice_in_dim(partial, first, block, 0)
            if dh or dr:
                part = swap(part, sizes, dr, dh * CORES, 0)
            part = part.astype(jnp.float32)
            total = part if total is None else total + part
    own = total.astype(jnp.bfloat16)
    line = jnp.concatenate([own] + [swap(own, sizes, d, 0, 0) for d in range(1, n_rows)], axis=0)
    loads = None
    for dk in range(n_groups):
        mine = [
            swap(line, sizes, 0, dh * CORES, dk) if dh or dk else line for dh in range(n_high)
        ]
        theirs = [swap(piece, sizes, 0, 1, 0) for piece in mine]
        firsts = [
            (which * n_high + (high ^ dh)) * n_rows * block
            for which in (core, 1 - core)
            for dh in range(n_high)
        ]
        loads = place_loads(
            mine + theirs, firsts, row, block, group ^ dk, n_groups, scale, loads
        )

    left = jnp.dot(mode_shapes, loads, preferred_element_type=jnp.float32).astype(jnp.bfloat16)
    panel = None
    columns = own_rows * n_groups
    for q in range(chunks):
        for dk in range(n_groups):
            piece = other[q][dk - 1] if dk else same[q]
            place = (group ^ dk) * chunks + q
            panel = place_panel(piece, loads, left, place, columns, panel)
    return panel


def solution(mesh):
    sizes = tuple(mesh.shape[axis] for axis in AXES)
    in_specs = (
        P(("prow", "pcol"), "pl"),
        P(None, ("prow", "pcol")),
        P(("prow", "pl"), None),
        P(),
        P(),
    )
    out_specs = P(("prow", "pl"), "pcol")
    return jax.shard_map(
        functools.partial(body, sizes), mesh=mesh, in_specs=in_specs, out_specs=out_specs, check_vma=False
    )
```

```python
import functools

import jax
import jax.numpy as jnp
from jax import lax
from jax.experimental import pallas as pl
from jax.experimental.pallas import tpu as pltpu
from jax.sharding import PartitionSpec as P

AXES = ("prow", "pcol", "pl")
CORES = 2
CHUNKS = (1, 1, 2, 2, 2)
AHEAD = 2
MIB = 1024 * 1024


def transfer_pair(natural_freq, damping):
    detuning = natural_freq * natural_freq - 1.0
    damper = 2.0 * damping * natural_freq
    modulus = detuning * detuning + damper * damper
    return detuning / modulus, -damper / modulus


def moves(sizes, source_of):
    rows, cols, groups = sizes
    pairs = []
    for i in range(rows):
        for j in range(cols):
            for k in range(groups):
                a, b, c = source_of(i, j, k)
                pairs.append(((a * cols + b) * groups + c, (i * cols + j) * groups + k))
    return pairs


def swap(array, sizes, di, dj, dk):
    return lax.ppermute(array, AXES, moves(sizes, lambda i, j, k: (i ^ di, j ^ dj, k ^ dk)))


def across(array, sizes, flip):
    return lax.ppermute(array, AXES, moves(sizes, lambda i, j, k: (j, i ^ flip, k)))


def cheap():
    return pl.CostEstimate(flops=1, bytes_accessed=1, transcendentals=0)


def after(array, *earlier):
    return pl.pallas_call(
        lambda *refs: None,
        in_specs=[pl.BlockSpec(memory_space=pl.ANY)] * (1 + len(earlier)),
        out_specs=pl.BlockSpec(memory_space=pl.ANY),
        out_shape=jax.ShapeDtypeStruct(array.shape, array.dtype),
        input_output_aliases={0: 0},
        cost_estimate=cheap(),
    )(array, *earlier)


def outer_rows(left_rows, right_rows):
    return lax.dot_general(
        left_rows, right_rows, (((1,), (1,)), ((), ())), preferred_element_type=jnp.float32
    )


def product_kernel(order, a, b, out):
    out[...] = jnp.dot(a[...], b[...], preferred_element_type=jnp.float32).astype(out.dtype)


def row_product(a, b, order, tile, dtype, limit):
    depth, wide = b.shape
    return pl.pallas_call(
        product_kernel,
        grid_spec=pltpu.PrefetchScalarGridSpec(
            num_scalar_prefetch=1,
            grid=(order.shape[0],),
            in_specs=[
                pl.BlockSpec((tile, depth), lambda g, order: (order[g], 0)),
                pl.BlockSpec((depth, wide), lambda g, order: (0, 0)),
            ],
            out_specs=pl.BlockSpec((tile, wide), lambda g, order: (g, 0)),
        ),
        out_shape=jax.ShapeDtypeStruct((order.shape[0] * tile, wide), dtype),
        compiler_params=pltpu.CompilerParams(vmem_limit_bytes=limit),
        cost_estimate=cheap(),
    )(order.astype(jnp.int32), a, b)


def load_kernel(rows, spots, scale, *refs):
    out = refs[-1]
    blocks = refs[: spots.shape[0] - 1]
    for at, block in enumerate(blocks):
        for part in range(block.shape[0] // rows):
            first = pl.multiple_of(spots[1 + at] + (spots[0] ^ part) * rows, rows)
            load = block[part * rows : (part + 1) * rows, :].astype(jnp.float32)
            out[pl.ds(first, rows), :] = (scale[0, pl.ds(first, rows), :] * load).astype(out.dtype)


def place_loads(blocks, firsts, own_row, rows, group, groups, scale, loads):
    modes, wide = scale.shape[1], blocks[0].shape[1]
    spots = jnp.stack([own_row, *firsts]).astype(jnp.int32)
    column = jnp.reshape(group, (1,)).astype(jnp.int32)
    given = [] if loads is None else [loads]
    return pl.pallas_call(
        lambda spots, column, *refs: load_kernel(rows, spots, *refs),
        grid_spec=pltpu.PrefetchScalarGridSpec(
            num_scalar_prefetch=2,
            grid=(2,),
            in_specs=[pl.BlockSpec((1, modes, 1), lambda g, spots, column: (g, 0, 0))]
            + [pl.BlockSpec(b.shape, lambda g, spots, column: (0, 0)) for b in blocks]
            + [pl.BlockSpec(memory_space=pl.ANY) for _ in given],
            out_specs=pl.BlockSpec((modes, wide), lambda g, spots, column: (0, g * groups + column[0])),
        ),
        out_shape=jax.ShapeDtypeStruct((modes, 2 * groups * wide), jnp.bfloat16),
        input_output_aliases={3 + len(blocks): 0} if given else {},
        compiler_params=pltpu.CompilerParams(vmem_limit_bytes=12 * MIB),
        cost_estimate=cheap(),
    )(spots, column, scale, *blocks, *given)


def panel_kernel(count, spots, *refs):
    lefts, rights, out = refs[:count], refs[count : 2 * count], refs[-1]
    depth = lefts[0].shape[1]

    def total(first):
        terms = [outer_rows(lefts[d ^ first][...], rights[d][...]) for d in range(count)]
        return functools.reduce(lambda a, b: a + b, terms)

    for first in range(count):
        @pl.when(spots[1] == first)
        def _():
            out[...] = total(first)


def place_panel(lefts, rights, first, place, columns, panel):
    rows, depth = lefts[0].shape
    chunk, count = rights[0].shape[0], len(lefts)
    given = [] if panel is None else [panel]
    tile = min(rows, 256)
    step = min(depth, 512)
    spots = jnp.stack([place, first]).astype(jnp.int32)
    return pl.pallas_call(
        functools.partial(panel_kernel, count),
        grid_spec=pltpu.PrefetchScalarGridSpec(
            num_scalar_prefetch=1,
            grid=(rows // tile,),
            in_specs=[pl.BlockSpec((tile, depth), lambda g, spots: (g, 0)) for _ in lefts]
            + [pl.BlockSpec((chunk, depth), lambda g, spots: (0, 0)) for _ in rights]
            + [pl.BlockSpec(memory_space=pl.ANY) for _ in given],
            out_specs=pl.BlockSpec((tile, chunk), lambda g, spots: (g, spots[0])),
        ),
        out_shape=jax.ShapeDtypeStruct((rows, columns), jnp.float32),
        input_output_aliases={1 + 2 * count: 0} if given else {},
        compiler_params=pltpu.CompilerParams(vmem_limit_bytes=24 * MIB),
        cost_estimate=pl.CostEstimate(
            flops=2 * rows * chunk * depth * count,
            bytes_accessed=2 * (rows + chunk) * depth * count + 4 * rows * chunk,
            transcendentals=0,
        ),
    )(spots, *lefts, *rights, *given)


def body(sizes, factor_cols, modal_at_loads, mode_shapes, natural_freq, damping):
    n_rows, n_cols, n_groups = sizes
    n_high = n_cols // CORES
    row, col, group = (lax.axis_index(axis) for axis in AXES)
    high, core = col // CORES, col % CORES
    scale = jnp.stack(transfer_pair(natural_freq, damping))[:, :, None]
    own_rows, modes = mode_shapes.shape

    part = factor_cols.shape[1] // n_high
    block = modes // CORES // n_rows
    order = row ^ jnp.arange(n_rows)
    sent = row_product(modal_at_loads, factor_cols, (1 - core) * n_rows + order, block, jnp.bfloat16, 56 * MIB)
    came = swap(sent, sizes, 0, 1, 0)
    here = row_product(modal_at_loads, factor_cols, core * n_rows + order, block, jnp.float32, 56 * MIB)
    total = here + came.astype(jnp.float32)
    own = None
    for dh in range(n_high):
        columns = lax.dynamic_slice_in_dim(total, (high ^ dh) * part, part, 1)
        for dr in range(n_rows):
            piece = columns[dr * block : (dr + 1) * block]
            if dh or dr:
                piece = swap(piece.astype(jnp.bfloat16), sizes, dr, dh * CORES, 0).astype(jnp.float32)
            own = piece if own is None else own + piece
    own = own.astype(jnp.bfloat16)
    loads = None
    for dk in range(n_groups):
        mine = [swap(own, sizes, dr, 0, dk) if dr or dk else own for dr in range(n_rows)]
        mine = jnp.concatenate(mine, axis=0)
        theirs = swap(mine, sizes, 0, 1, 0)
        firsts = [which * n_rows * block for which in (core, 1 - core)]
        loads = place_loads([mine, theirs], firsts, row, block, group ^ dk, n_groups, scale, loads)

    tile = min(own_rows, 256)
    left = row_product(mode_shapes, loads, jnp.arange(own_rows // tile), tile, jnp.bfloat16, 56 * MIB)
    half = own_rows // CORES
    lefts = [left]
    for dh in range(1, n_high):
        sent = lax.dynamic_slice_in_dim(left, core * half, half, 0)
        came = swap(sent, sizes, 0, dh * CORES, 0)
        rest = swap(came, sizes, 0, 1, 0)
        lefts.append(
            jnp.where(core == 0, jnp.concatenate([came, rest], 0), jnp.concatenate([rest, came], 0))
        )

    unit = max(own_rows // sum(CHUNKS), min(own_rows, 128))
    spans, first = [], 0
    while first < own_rows:
        size = min(CHUNKS[min(len(spans), len(CHUNKS) - 1)] * unit, own_rows - first)
        spans.append((first, size))
        first += size

    landed, others = [], []
    for at, (first, size) in enumerate(spans):
        piece = left[first : first + size]
        if at >= AHEAD:
            piece = after(piece, *landed[at - AHEAD])
        landed.append([across(piece, sizes, dh * CORES) for dh in range(n_high)])
        others.append([[swap(p, sizes, 0, 0, dk) for p in landed[at]] for dk in range(1, n_groups)])

    panel, columns = None, own_rows * n_groups
    turn = (row // CORES) ^ high
    for at, (first, size) in enumerate(spans):
        for dk in range(n_groups):
            rights = others[at][dk - 1] if dk else landed[at]
            place = (group ^ dk) * (own_rows // size) + first // size
            panel = place_panel(lefts, rights, turn, place, columns, panel)
    return panel


def solution(mesh):
    sizes = tuple(mesh.shape[axis] for axis in AXES)
    in_specs = (
        P(("prow", "pcol"), "pl"),
        P(None, ("prow", "pcol")),
        P(("prow", "pl"), None),
        P(),
        P(),
    )
    out_specs = P(("prow", "pl"), "pcol")
    return jax.shard_map(
        functools.partial(body, sizes), mesh=mesh, in_specs=in_specs, out_specs=out_specs, check_vma=False
    )
```

```python
import functools

import jax
import jax.numpy as jnp
from jax import lax
from jax.experimental import pallas as pl
from jax.experimental.pallas import tpu as pltpu
from jax.sharding import PartitionSpec as P

AXES = ("prow", "pcol", "pl")
CORES = 2
CHUNKS = (4,4)
UNIT = 4
AHEAD = 1
LEFT = 0
MIB = 1024 * 1024


def transfer_pair(natural_freq, damping):
    detuning = natural_freq * natural_freq - 1.0
    damper = 2.0 * damping * natural_freq
    modulus = detuning * detuning + damper * damper
    return detuning / modulus, -damper / modulus


def moves(sizes, source_of):
    rows, cols, groups = sizes
    pairs = []
    for i in range(rows):
        for j in range(cols):
            for k in range(groups):
                a, b, c = source_of(i, j, k)
                pairs.append(((a * cols + b) * groups + c, (i * cols + j) * groups + k))
    return pairs


def swap(array, sizes, di, dj, dk):
    return lax.ppermute(array, AXES, moves(sizes, lambda i, j, k: (i ^ di, j ^ dj, k ^ dk)))


def across(array, sizes, flip):
    return lax.ppermute(array, AXES, moves(sizes, lambda i, j, k: (j, i ^ flip, k)))


def cheap():
    return pl.CostEstimate(flops=1, bytes_accessed=1, transcendentals=0)


def after(array, *earlier):
    return pl.pallas_call(
        lambda *refs: None,
        in_specs=[pl.BlockSpec(memory_space=pl.ANY)] * (1 + len(earlier)),
        out_specs=pl.BlockSpec(memory_space=pl.ANY),
        out_shape=jax.ShapeDtypeStruct(array.shape, array.dtype),
        input_output_aliases={0: 0},
        cost_estimate=cheap(),
    )(array, *earlier)


def outer_rows(left_rows, right_rows):
    return lax.dot_general(
        left_rows, right_rows, (((1,), (1,)), ((), ())), preferred_element_type=jnp.float32
    )


def product_kernel(a, b, out):
    out[...] = jnp.dot(a[...], b[...], preferred_element_type=jnp.float32).astype(out.dtype)


def row_product(a, b, tile, limit):
    rows, depth = a.shape
    wide = b.shape[1]
    return pl.pallas_call(
        product_kernel,
        grid=(rows // tile,),
        in_specs=[
            pl.BlockSpec((tile, depth), lambda g: (g, 0)),
            pl.BlockSpec((depth, wide), lambda g: (0, 0)),
        ],
        out_specs=pl.BlockSpec((tile, wide), lambda g: (g, 0)),
        out_shape=jax.ShapeDtypeStruct((rows, wide), jnp.bfloat16),
        compiler_params=pltpu.CompilerParams(vmem_limit_bytes=limit),
        cost_estimate=cheap(),
    )(a, b)


def load_kernel(rows, spots, scale, *refs):
    out = refs[-1]
    blocks = refs[: spots.shape[0] - 1]
    for at, block in enumerate(blocks):
        for part in range(block.shape[0] // rows):
            first = pl.multiple_of(spots[1 + at] + (spots[0] ^ part) * rows, rows)
            load = block[part * rows : (part + 1) * rows, :].astype(jnp.float32)
            out[pl.ds(first, rows), :] = (scale[0, pl.ds(first, rows), :] * load).astype(out.dtype)


def place_loads(blocks, firsts, own_row, rows, group, groups, scale, loads):
    modes, wide = scale.shape[1], blocks[0].shape[1]
    spots = jnp.stack([own_row, *firsts]).astype(jnp.int32)
    column = jnp.reshape(group, (1,)).astype(jnp.int32)
    given = [] if loads is None else [loads]
    return pl.pallas_call(
        lambda spots, column, *refs: load_kernel(rows, spots, *refs),
        grid_spec=pltpu.PrefetchScalarGridSpec(
            num_scalar_prefetch=2,
            grid=(2,),
            in_specs=[pl.BlockSpec((1, modes, 1), lambda g, spots, column: (g, 0, 0))]
            + [pl.BlockSpec(b.shape, lambda g, spots, column: (0, 0)) for b in blocks]
            + [pl.BlockSpec(memory_space=pl.ANY) for _ in given],
            out_specs=pl.BlockSpec((modes, wide), lambda g, spots, column: (0, g * groups + column[0])),
        ),
        out_shape=jax.ShapeDtypeStruct((modes, 2 * groups * wide), jnp.bfloat16),
        input_output_aliases={3 + len(blocks): 0} if given else {},
        compiler_params=pltpu.CompilerParams(vmem_limit_bytes=12 * MIB),
        cost_estimate=cheap(),
    )(spots, column, scale, *blocks, *given)


def panel_kernel(count, shape, spots, left, *refs):
    out = refs[-2]
    for unit, pieces in enumerate(shape):
        spans, refs = refs[: pieces * count], refs[pieces * count :]

        def fill(spans=spans, pieces=pieces):
            rights = [
                jnp.concatenate([spans[p * count + d][...] for d in range(count)], axis=1)
                for p in range(pieces)
            ]
            out[...] = outer_rows(left[...], jnp.concatenate(rights, axis=0))

        if len(shape) == 1:
            fill()
        else:
            pl.when(pl.program_id(0) == unit)(fill)


def place_panel(left, units, places, columns, panel, *earlier):
    rows, count = left.shape[0], len(units[0][0])
    chunk = sum(piece[0].shape[0] for piece in units[0])
    shape = tuple(len(unit) for unit in units)
    rights = [array for unit in units for piece in unit for array in piece]
    given = ([] if panel is None else [panel]) + list(earlier)
    whole = pl.BlockSpec(memory_space=pltpu.VMEM)
    return pl.pallas_call(
        functools.partial(panel_kernel, count, shape),
        grid_spec=pltpu.PrefetchScalarGridSpec(
            num_scalar_prefetch=1,
            grid=(len(units),),
            in_specs=[whole] * (1 + len(rights)) + [pl.BlockSpec(memory_space=pl.ANY) for _ in given],
            out_specs=[
                pl.BlockSpec((rows, chunk), lambda g, spots: (0, spots[g])),
                pl.BlockSpec(memory_space=pl.ANY),
            ],
        ),
        out_shape=[
            jax.ShapeDtypeStruct((rows, columns), jnp.float32),
            jax.ShapeDtypeStruct((8, 128), jnp.float32),
        ],
        input_output_aliases={} if panel is None else {2 + len(rights): 0},
        compiler_params=pltpu.CompilerParams(vmem_limit_bytes=12 * MIB),
        cost_estimate=cheap(),
    )(jnp.stack(places).astype(jnp.int32), left, *rights, *given)


def body(sizes, factor_cols, modal_at_loads, mode_shapes, natural_freq, damping):
    n_rows, n_cols, n_groups = sizes
    n_high = n_cols // CORES
    row, col, group = (lax.axis_index(axis) for axis in AXES)
    high, core = col // CORES, col % CORES
    scale = jnp.stack(transfer_pair(natural_freq, damping))[:, :, None]
    own_rows, modes = mode_shapes.shape

    part = factor_cols.shape[1] // n_high
    block = modes // CORES // n_rows
    half = block * n_rows
    away = lax.dynamic_slice_in_dim(modal_at_loads, (1 - core) * half, half, 0)
    here = lax.dynamic_slice_in_dim(modal_at_loads, core * half, half, 0)
    sent = jnp.dot(away, factor_cols, preferred_element_type=jnp.float32).astype(jnp.bfloat16)
    came = swap(sent, sizes, 0, 1, 0)
    total = jnp.dot(here, factor_cols, preferred_element_type=jnp.float32) + came.astype(jnp.float32)
    total = total.astype(jnp.bfloat16)
    own = None
    for dh in range(n_high):
        for dr in range(n_rows):
            piece = lax.dynamic_slice(total, ((row ^ dr) * block, (high ^ dh) * part), (block, part))
            if dh or dr:
                piece = swap(piece, sizes, dr, dh * CORES, 0)
            piece = piece.astype(jnp.float32)
            own = piece if own is None else own + piece
    own = own.astype(jnp.bfloat16)
    loads = None
    for dk in range(n_groups):
        mine = [swap(own, sizes, dr, 0, dk) if dr or dk else own for dr in range(n_rows)]
        mine = jnp.concatenate(mine, axis=0)
        theirs = swap(mine, sizes, 0, 1, 0)
        firsts = [which * n_rows * block for which in (core, 1 - core)]
        loads = place_loads([mine, theirs], firsts, row, block, group ^ dk, n_groups, scale, loads)

    tile, width = min(own_rows, 256), loads.shape[1]
    left = row_product(mode_shapes, loads, tile, 12 * MIB if width <= modes else 56 * MIB)
    lefts = []

    unit = max(own_rows // sum(CHUNKS), min(own_rows, 128))
    spans, first = [], 0
    while first < own_rows:
        size = min(CHUNKS[min(len(spans), len(CHUNKS) - 1)] * unit, own_rows - first)
        spans.append((first, size))
        first += size

    size = min(UNIT * unit, own_rows)
    members = [
        [at for at, (first, _) in enumerate(spans) if first // size == which]
        for which in range(own_rows // size)
    ]
    n, m = len(spans), len(members)
    landed, others = [[] for _ in spans], [None] * n
    panel, columns = None, own_rows * n_groups
    turn = (row // CORES) ^ high

    def launch(at):
        first, count = spans[at]
        for dh in range(n_high):
            piece = left[first : first + count]
            if at >= AHEAD:
                piece = after(piece, landed[at - AHEAD][dh])
            landed[at].append(across(piece, sizes, dh * CORES))

    def widen(*earlier):
        half = own_rows // CORES
        whole = [left]
        for dh in range(1, n_high):
            sent = lax.dynamic_slice_in_dim(left, core * half, half, 0)
            came = swap(after(sent, *earlier), sizes, 0, dh * CORES, 0)
            rest = swap(came, sizes, 0, 1, 0)
            whole.append(
                jnp.where(core == 0, jnp.concatenate([came, rest], 0), jnp.concatenate([rest, came], 0))
            )
        joined = [
            jnp.concatenate([whole[d ^ first] for d in range(n_high)], axis=1) for first in range(n_high)
        ]
        wide = joined[-1]
        for first in range(n_high - 1):
            wide = jnp.where(turn == first, joined[first], wide)
        lefts.append(wide)

    def relay(at):
        if at:
            landed[at] = [
                after(piece, *[pieces[dh] for pieces in others[at - 1]])
                for dh, piece in enumerate(landed[at])
            ]
        others[at] = [[swap(p, sizes, 0, 0, dk) for p in landed[at]] for dk in range(1, n_groups)]

    def fill(wanted, *earlier):
        nonlocal panel
        units = [
            [others[at][dk - 1] if dk else landed[at] for at in members[which]] for which, dk in wanted
        ]
        places = [(group ^ dk) * len(members) + which for which, dk in wanted]
        panel, token = place_panel(lefts[0], units, places, columns, panel, *earlier)
        return token

    for at in range(n):
        launch(at)
        relay(at)
        if at == min(LEFT, n - 1):
            widen(*landed[at])
    pairs = [(which, dk) for dk in range(n_groups) for which in range(m)]
    last = [pair for pair in pairs if pair[1] and members[pair[0]][-1] == n - 1]
    first = [pair for pair in pairs if pair not in last]
    if first:
        fill(first)
    if last:
        fill(last)
    return panel


def solution(mesh):
    sizes = tuple(mesh.shape[axis] for axis in AXES)
    in_specs = (
        P(("prow", "pcol"), "pl"),
        P(None, ("prow", "pcol")),
        P(("prow", "pl"), None),
        P(),
        P(),
    )
    out_specs = P(("prow", "pl"), "pcol")
    return jax.shard_map(
        functools.partial(body, sizes), mesh=mesh, in_specs=in_specs, out_specs=out_specs, check_vma=False
    )
```

```python
import functools

import jax
import jax.numpy as jnp
from jax import lax
from jax.experimental import pallas as pl
from jax.experimental.pallas import tpu as pltpu
from jax.sharding import PartitionSpec as P

AXES = ("prow", "pcol", "pl")
CORES = 2
UNITS = 4
LAST = 1
PROJECT = 48
MIB = 1024 * 1024


def transfer_pair(natural_freq, damping):
    detuning = natural_freq * natural_freq - 1.0
    damper = 2.0 * damping * natural_freq
    modulus = detuning * detuning + damper * damper
    return detuning / modulus, -damper / modulus


def moves(sizes, source_of):
    rows, cols, groups = sizes
    pairs = []
    for i in range(rows):
        for j in range(cols):
            for k in range(groups):
                a, b, c = source_of(i, j, k)
                pairs.append(((a * cols + b) * groups + c, (i * cols + j) * groups + k))
    return pairs


def swap(array, sizes, di, dj, dk):
    return lax.ppermute(array, AXES, moves(sizes, lambda i, j, k: (i ^ di, j ^ dj, k ^ dk)))


def across(array, sizes, flip):
    return lax.ppermute(array, AXES, moves(sizes, lambda i, j, k: (j, i ^ flip, k)))


def cheap():
    return pl.CostEstimate(flops=1, bytes_accessed=1, transcendentals=0)


def after(array, *earlier):
    return pl.pallas_call(
        lambda *refs: None,
        in_specs=[pl.BlockSpec(memory_space=pl.ANY)] * (1 + len(earlier)),
        out_specs=pl.BlockSpec(memory_space=pl.ANY),
        out_shape=jax.ShapeDtypeStruct(array.shape, array.dtype),
        input_output_aliases={0: 0},
        cost_estimate=cheap(),
    )(array, *earlier)


def outer_rows(left_rows, right_rows):
    return lax.dot_general(
        left_rows, right_rows, (((1,), (1,)), ((), ())), preferred_element_type=jnp.float32
    )


def gather_kernel(rows, wide, spots, *refs):
    out = refs[-1]
    count = len(refs) - 1
    parts = out.shape[0] // rows
    for at in range(count):
        dk, dr = divmod(at, parts)
        first = pl.multiple_of((spots[0] ^ dr) * rows, rows)
        left = pl.multiple_of((spots[1] ^ dk) * wide, wide)
        out[pl.ds(first, rows), pl.ds(left, wide)] = refs[at][...]


def gather_loads(blocks, row, group, parts):
    rows, wide = blocks[0].shape
    whole = pl.BlockSpec(memory_space=pltpu.VMEM)
    shape = (rows * parts, wide * (len(blocks) // parts))
    return pl.pallas_call(
        functools.partial(gather_kernel, rows, wide),
        in_specs=[pl.BlockSpec(memory_space=pltpu.SMEM)] + [whole] * len(blocks),
        out_specs=whole,
        out_shape=jax.ShapeDtypeStruct(shape, jnp.bfloat16),
        compiler_params=pltpu.CompilerParams(vmem_limit_bytes=12 * MIB),
        cost_estimate=cheap(),
    )(jnp.stack([row, group]).astype(jnp.int32), *blocks)


def project_kernel(spots, mine, theirs, scale, shapes, out, loads):
    half, wide = mine.shape

    @pl.when(pl.program_id(0) == 0)
    def _():
        strip = min(wide, 256)
        for block, core in ((mine, spots[0]), (theirs, 1 - spots[0])):
            first = pl.multiple_of(core * half, half)

            @pl.loop(0, wide // strip)
            def _(at, block=block, first=first):
                left = pl.multiple_of(at * strip, strip)
                load = block[:, pl.ds(left, strip)].astype(jnp.float32)
                for part in range(2):
                    scaled = scale[part, pl.ds(first, half), :] * load
                    place = pl.multiple_of(part * wide + at * strip, strip)
                    loads[pl.ds(first, half), pl.ds(place, strip)] = scaled.astype(loads.dtype)

    out[...] = jnp.dot(shapes[...], loads[...], preferred_element_type=jnp.float32).astype(out.dtype)


def project(mode_shapes, mine, theirs, scale, core, first, last, tile):
    modes, wide = mode_shapes.shape[1], 2 * mine.shape[1]
    whole = pl.BlockSpec(memory_space=pltpu.VMEM)
    return pl.pallas_call(
        project_kernel,
        grid_spec=pltpu.PrefetchScalarGridSpec(
            num_scalar_prefetch=1,
            grid=(last - first,),
            in_specs=[whole] * 3 + [pl.BlockSpec((tile, modes), lambda g, spots: (first + g, 0))],
            out_specs=pl.BlockSpec((tile, wide), lambda g, spots: (g, 0)),
            scratch_shapes=[pltpu.VMEM((modes, wide), jnp.bfloat16)],
        ),
        out_shape=jax.ShapeDtypeStruct((tile * (last - first), wide), jnp.bfloat16),
        compiler_params=pltpu.CompilerParams(vmem_limit_bytes=PROJECT * MIB),
        cost_estimate=cheap(),
    )(jnp.reshape(core, (1,)).astype(jnp.int32), mine, theirs, scale, mode_shapes)


def widen_kernel(sets, spots, *refs):
    out, own, refs = refs[-1], refs[: len(sets)], refs[len(sets) : -1]
    deep = own[0].shape[1]

    def lay(array, spans, place):
        left, low = pl.multiple_of(place * deep, deep), 0
        for first, count in spans:
            out[first : first + count, pl.ds(left, deep)] = array[low : low + count, :]
            low += count

    for at, spans in enumerate(sets):
        lay(own[at], spans, spots[1])
    for core in range(len(sets)):

        @pl.when(spots[0] == core)
        def _(core=core):
            for at in range(0, len(refs), len(sets)):
                place = spots[1] ^ (at // len(sets) + 1)
                for d in range(len(sets)):
                    lay(refs[at + d], sets[core ^ d], place)


def widen_left(sets, own, others, core, turn, rows):
    whole = pl.BlockSpec(memory_space=pltpu.VMEM)
    deep = own[0].shape[1]
    wide = deep * (1 + len(others) // len(sets))
    return pl.pallas_call(
        functools.partial(widen_kernel, sets),
        in_specs=[pl.BlockSpec(memory_space=pltpu.SMEM)] + [whole] * (len(own) + len(others)),
        out_specs=whole,
        out_shape=jax.ShapeDtypeStruct((rows, wide), jnp.bfloat16),
        compiler_params=pltpu.CompilerParams(vmem_limit_bytes=12 * MIB),
        cost_estimate=cheap(),
    )(jnp.stack([core, turn]).astype(jnp.int32), *own, *others)


def panel_kernel(chunk, count, spots, left, *refs):
    first = pl.multiple_of(pl.program_id(0) * chunk, chunk)
    right = jnp.concatenate([piece[pl.ds(first, chunk), :] for piece in refs[:count]], axis=1)
    refs[-1][...] = outer_rows(left[...], right)


def place_panel(left, pieces, chunk, places, columns, panel):
    rows = left.shape[0]
    given = [] if panel is None else [panel]
    whole = pl.BlockSpec(memory_space=pltpu.VMEM)
    return pl.pallas_call(
        functools.partial(panel_kernel, chunk, len(pieces)),
        grid_spec=pltpu.PrefetchScalarGridSpec(
            num_scalar_prefetch=1,
            grid=(len(places),),
            in_specs=[whole] * (1 + len(pieces)) + [pl.BlockSpec(memory_space=pl.ANY) for _ in given],
            out_specs=pl.BlockSpec((rows, chunk), lambda g, spots: (0, spots[g])),
        ),
        out_shape=jax.ShapeDtypeStruct((rows, columns), jnp.float32),
        input_output_aliases={2 + len(pieces): 0} if given else {},
        compiler_params=pltpu.CompilerParams(vmem_limit_bytes=12 * MIB),
        cost_estimate=cheap(),
    )(jnp.stack(places).astype(jnp.int32), left, *pieces, *given)


def body(sizes, factor_cols, modal_at_loads, mode_shapes, natural_freq, damping):
    n_rows, n_cols, n_groups = sizes
    n_high = n_cols // CORES
    row, col, group = (lax.axis_index(axis) for axis in AXES)
    high, core = col // CORES, col % CORES
    scale = jnp.stack(transfer_pair(natural_freq, damping))[:, :, None]
    own_rows, modes = mode_shapes.shape

    part = factor_cols.shape[1] // n_high
    block = modes // CORES // n_rows
    half = block * n_rows
    away = lax.dynamic_slice_in_dim(modal_at_loads, (1 - core) * half, half, 0)
    here = lax.dynamic_slice_in_dim(modal_at_loads, core * half, half, 0)
    sent = jnp.dot(away, factor_cols, preferred_element_type=jnp.float32).astype(jnp.bfloat16)
    came = swap(sent, sizes, 0, 1, 0)
    total = jnp.dot(here, factor_cols, preferred_element_type=jnp.float32) + came.astype(jnp.float32)
    total = total.astype(jnp.bfloat16)
    own = None
    for dh in range(n_high):
        for dr in range(n_rows):
            piece = lax.dynamic_slice(total, ((row ^ dr) * block, (high ^ dh) * part), (block, part))
            if dh or dr:
                piece = swap(piece, sizes, dr, dh * CORES, 0)
            piece = piece.astype(jnp.float32)
            own = piece if own is None else own + piece
    own = own.astype(jnp.bfloat16)
    blocks = [
        swap(own, sizes, dr, 0, dk) if dr or dk else own for dk in range(n_groups) for dr in range(n_rows)
    ]
    mine = gather_loads(blocks, row, group, n_rows)
    theirs = swap(mine, sizes, 0, 1, 0)

    unit = max(own_rows // UNITS, min(own_rows, 128))
    units = own_rows // unit
    bounds = (0, 1, units - 1, units) if units > 2 else tuple(range(units + 1))
    lots = [
        project(mode_shapes, mine, theirs, scale, core, first, last, unit)
        for first, last in zip(bounds[:-1], bounds[1:])
    ]
    size = own_rows // CORES
    if units == 4:
        sets = (((0, unit), (3 * unit, unit)), ((unit, 2 * unit),))
        halves = [jnp.concatenate([lots[0], lots[2]], axis=0), lots[1]]
    else:
        sets = tuple(((first, size),) for first in range(0, own_rows, size))
        left = jnp.concatenate(lots, axis=0) if len(lots) > 1 else lots[0]
        halves = [left[first : first + size] for first in range(0, own_rows, size)]

    def cross(rows, earlier):
        pair = []
        for dh in range(n_high):
            held = after(rows, *earlier[dh]) if earlier else rows
            pair.append(across(held, sizes, dh * CORES))
        return pair

    def relay(pair, earlier):
        if earlier:
            pair = [after(rows, *[sent[dh] for sent in earlier]) for dh, rows in enumerate(pair)]
        return pair, [[swap(rows, sizes, 0, 0, dk) for rows in pair] for dk in range(1, n_groups)]

    landed = cross(lots[0], [])
    both = []
    if units > 2:
        both = [lots[2]] + [swap(lots[2], sizes, 0, 0, dk) for dk in range(1, n_groups)]
    landed, others = relay(landed, [])
    pieces = [(landed, others, 0)]

    away = jnp.where(core == 0, halves[0], halves[1])
    widened = [swap(after(away, *landed), sizes, 0, dh * CORES, 0) for dh in range(1, n_high)]
    done = list(widened) + [rows for sent in others for rows in sent]

    crossed = landed
    if units > 1:
        crossed = cross(lots[1], [[rows] for rows in crossed])
        done += crossed
        landed, others = relay(crossed, others)
        pieces.append((landed, others, 1))
    if units > 2:
        landed = cross(jnp.concatenate(both, axis=0), [done] * n_high)
        pieces.append((landed, None, units - 1))

    rests = []
    for came in widened:
        came = after(came, *crossed)
        rests += [came, swap(came, sizes, 0, 1, 0)]
    turn = (row // CORES) ^ high
    wide = widen_left(sets, halves, rests, core, turn, own_rows)

    panel, columns = None, own_rows * n_groups

    def fill(pair, first, shifts):
        nonlocal panel
        count = pair[0].shape[0] // unit // len(shifts)
        places = [(group ^ dk) * units + first + at for dk in shifts for at in range(count)]
        panel = place_panel(wide, pair, unit, places, columns, panel)

    for pair, sent, first in pieces:
        if sent is not None:
            fill(pair, first, [0])
    for pair, sent, first in pieces[:1]:
        for dk in range(1, n_groups):
            fill(sent[dk - 1], first, [dk])
    for pair, sent, first in pieces[LAST:] + pieces[1:LAST]:
        if sent is None:
            fill(pair, first, list(range(n_groups)))
        else:
            for dk in range(1, n_groups):
                fill(sent[dk - 1], first, [dk])
    return panel


def solution(mesh):
    sizes = tuple(mesh.shape[axis] for axis in AXES)
    in_specs = (
        P(("prow", "pcol"), "pl"),
        P(None, ("prow", "pcol")),
        P(("prow", "pl"), None),
        P(),
        P(),
    )
    out_specs = P(("prow", "pl"), "pcol")
    return jax.shard_map(
        functools.partial(body, sizes), mesh=mesh, in_specs=in_specs, out_specs=out_specs, check_vma=False
    )
```

```python
import functools

import jax
import jax.numpy as jnp
from jax import lax
from jax.experimental import pallas as pl
from jax.experimental.pallas import tpu as pltpu
from jax.sharding import PartitionSpec as P

AXES = ("prow", "pcol", "pl")
CORES = 2
UNITS = 4
LAST = 1
PROJECT = 48
MIB = 1024 * 1024


def transfer_pair(natural_freq, damping):
    detuning = natural_freq * natural_freq - 1.0
    damper = 2.0 * damping * natural_freq
    modulus = detuning * detuning + damper * damper
    return detuning / modulus, -damper / modulus


def moves(sizes, source_of):
    rows, cols, groups = sizes
    pairs = []
    for i in range(rows):
        for j in range(cols):
            for k in range(groups):
                a, b, c = source_of(i, j, k)
                pairs.append(((a * cols + b) * groups + c, (i * cols + j) * groups + k))
    return pairs


def swap(array, sizes, di, dj, dk):
    return lax.ppermute(array, AXES, moves(sizes, lambda i, j, k: (i ^ di, j ^ dj, k ^ dk)))


def across(array, sizes, flip):
    return lax.ppermute(array, AXES, moves(sizes, lambda i, j, k: (j, i ^ flip, k)))


def cheap():
    return pl.CostEstimate(flops=1, bytes_accessed=1, transcendentals=0)


def after(array, *earlier):
    return pl.pallas_call(
        lambda *refs: None,
        in_specs=[pl.BlockSpec(memory_space=pl.ANY)] * (1 + len(earlier)),
        out_specs=pl.BlockSpec(memory_space=pl.ANY),
        out_shape=jax.ShapeDtypeStruct(array.shape, array.dtype),
        input_output_aliases={0: 0},
        cost_estimate=cheap(),
    )(array, *earlier)


def outer_rows(left_rows, right_rows):
    return lax.dot_general(
        left_rows, right_rows, (((1,), (1,)), ((), ())), preferred_element_type=jnp.float32
    )


def gather_kernel(rows, wide, spots, *refs):
    out = refs[-1]
    count = len(refs) - 1
    parts = out.shape[0] // rows
    for at in range(count):
        dk, dr = divmod(at, parts)
        first = pl.multiple_of((spots[0] ^ dr) * rows, rows)
        left = pl.multiple_of((spots[1] ^ dk) * wide, wide)
        out[pl.ds(first, rows), pl.ds(left, wide)] = refs[at][...]


def gather_loads(blocks, row, group, parts):
    rows, wide = blocks[0].shape
    whole = pl.BlockSpec(memory_space=pltpu.VMEM)
    shape = (rows * parts, wide * (len(blocks) // parts))
    return pl.pallas_call(
        functools.partial(gather_kernel, rows, wide),
        in_specs=[pl.BlockSpec(memory_space=pltpu.SMEM)] + [whole] * len(blocks),
        out_specs=whole,
        out_shape=jax.ShapeDtypeStruct(shape, jnp.bfloat16),
        compiler_params=pltpu.CompilerParams(vmem_limit_bytes=12 * MIB),
        cost_estimate=cheap(),
    )(jnp.stack([row, group]).astype(jnp.int32), *blocks)


def project_kernel(spots, mine, theirs, scale, shapes, out, loads):
    half, wide = mine.shape

    @pl.when(pl.program_id(0) == 0)
    def _():
        strip = min(wide, 256)
        for block, core in ((mine, spots[0]), (theirs, 1 - spots[0])):
            first = pl.multiple_of(core * half, half)

            @pl.loop(0, wide // strip)
            def _(at, block=block, first=first):
                left = pl.multiple_of(at * strip, strip)
                load = block[:, pl.ds(left, strip)].astype(jnp.float32)
                for part in range(2):
                    scaled = scale[part, pl.ds(first, half), :] * load
                    place = pl.multiple_of(part * wide + at * strip, strip)
                    loads[pl.ds(first, half), pl.ds(place, strip)] = scaled.astype(loads.dtype)

    out[...] = jnp.dot(shapes[...], loads[...], preferred_element_type=jnp.float32).astype(out.dtype)


def project(mode_shapes, mine, theirs, scale, core, first, last, tile):
    modes, wide = mode_shapes.shape[1], 2 * mine.shape[1]
    whole = pl.BlockSpec(memory_space=pltpu.VMEM)
    return pl.pallas_call(
        project_kernel,
        grid_spec=pltpu.PrefetchScalarGridSpec(
            num_scalar_prefetch=1,
            grid=(last - first,),
            in_specs=[whole] * 3 + [pl.BlockSpec((tile, modes), lambda g, spots: (first + g, 0))],
            out_specs=pl.BlockSpec((tile, wide), lambda g, spots: (g, 0)),
            scratch_shapes=[pltpu.VMEM((modes, wide), jnp.bfloat16)],
        ),
        out_shape=jax.ShapeDtypeStruct((tile * (last - first), wide), jnp.bfloat16),
        compiler_params=pltpu.CompilerParams(vmem_limit_bytes=PROJECT * MIB),
        cost_estimate=cheap(),
    )(jnp.reshape(core, (1,)).astype(jnp.int32), mine, theirs, scale, mode_shapes)


def widen_kernel(sets, spots, *refs):
    out, own, refs = refs[-1], refs[: len(sets)], refs[len(sets) : -1]
    deep = own[0].shape[1]

    def lay(array, spans, place):
        left, low = pl.multiple_of(place * deep, deep), 0
        for first, count in spans:
            out[first : first + count, pl.ds(left, deep)] = array[low : low + count, :]
            low += count

    for at, spans in enumerate(sets):
        lay(own[at], spans, spots[1])
    for core in range(len(sets)):

        @pl.when(spots[0] == core)
        def _(core=core):
            for at in range(0, len(refs), len(sets)):
                place = spots[1] ^ (at // len(sets) + 1)
                for d in range(len(sets)):
                    lay(refs[at + d], sets[core ^ d], place)


def widen_left(sets, own, others, core, turn, rows):
    whole = pl.BlockSpec(memory_space=pltpu.VMEM)
    deep = own[0].shape[1]
    wide = deep * (1 + len(others) // len(sets))
    return pl.pallas_call(
        functools.partial(widen_kernel, sets),
        in_specs=[pl.BlockSpec(memory_space=pltpu.SMEM)] + [whole] * (len(own) + len(others)),
        out_specs=whole,
        out_shape=jax.ShapeDtypeStruct((rows, wide), jnp.bfloat16),
        compiler_params=pltpu.CompilerParams(vmem_limit_bytes=12 * MIB),
        cost_estimate=cheap(),
    )(jnp.stack([core, turn]).astype(jnp.int32), *own, *others)


def panel_kernel(chunk, count, spots, left, *refs):
    first = pl.multiple_of(pl.program_id(0) * chunk, chunk)
    right = jnp.concatenate([piece[pl.ds(first, chunk), :] for piece in refs[:count]], axis=1)
    refs[-1][...] = outer_rows(left[...], right)


def place_panel(left, pieces, chunk, places, columns, panel):
    rows = left.shape[0]
    given = [] if panel is None else [panel]
    whole = pl.BlockSpec(memory_space=pltpu.VMEM)
    return pl.pallas_call(
        functools.partial(panel_kernel, chunk, len(pieces)),
        grid_spec=pltpu.PrefetchScalarGridSpec(
            num_scalar_prefetch=1,
            grid=(len(places),),
            in_specs=[whole] * (1 + len(pieces)) + [pl.BlockSpec(memory_space=pl.ANY) for _ in given],
            out_specs=pl.BlockSpec((rows, chunk), lambda g, spots: (0, spots[g])),
        ),
        out_shape=jax.ShapeDtypeStruct((rows, columns), jnp.float32),
        input_output_aliases={2 + len(pieces): 0} if given else {},
        compiler_params=pltpu.CompilerParams(vmem_limit_bytes=12 * MIB),
        cost_estimate=cheap(),
    )(jnp.stack(places).astype(jnp.int32), left, *pieces, *given)


def body(sizes, factor_cols, modal_at_loads, mode_shapes, natural_freq, damping):
    n_rows, n_cols, n_groups = sizes
    n_high = n_cols // CORES
    row, col, group = (lax.axis_index(axis) for axis in AXES)
    high, core = col // CORES, col % CORES
    scale = jnp.stack(transfer_pair(natural_freq, damping))[:, :, None]
    own_rows, modes = mode_shapes.shape

    part = factor_cols.shape[1] // n_high
    block = modes // CORES // n_rows
    half = block * n_rows
    near = n_rows // 2
    size = half // 2

    def partial(which, side):
        rows = lax.dynamic_slice_in_dim(modal_at_loads, which * half + side * size, size, 0)
        return jnp.dot(rows, factor_cols, preferred_element_type=jnp.float32)

    own = None
    for part_of, side in ((1, (row // near) ^ 1), (0, row // near)):
        came = swap(partial(1 - core, side).astype(jnp.bfloat16), sizes, 0, 1, 0)
        total = (partial(core, side) + came.astype(jnp.float32)).astype(jnp.bfloat16)
        for dh in reversed(range(n_high)):
            for dr in reversed(range(near)):
                first = ((row ^ dr) % near) * block
                piece = lax.dynamic_slice(total, (first, (high ^ dh) * part), (block, part))
                if dh or dr or part_of:
                    piece = swap(piece, sizes, dr + part_of * near, dh * CORES, 0)
                piece = piece.astype(jnp.float32)
                own = piece if own is None else own + piece
    own = own.astype(jnp.bfloat16)
    line = [swap(own, sizes, dr, 0, 0) if dr else own for dr in range(n_rows)]
    blocks = list(line)
    for dk in range(1, n_groups):
        blocks += [swap(piece, sizes, 0, 0, dk) for piece in line]
    mine = gather_loads(blocks, row, group, n_rows)
    theirs = swap(mine, sizes, 0, 1, 0)

    unit = max(own_rows // UNITS, min(own_rows, 128))
    units = own_rows // unit
    bounds = (0, 1, units - 1, units) if units > 2 else tuple(range(units + 1))
    lots = [
        project(mode_shapes, mine, theirs, scale, core, first, last, unit)
        for first, last in zip(bounds[:-1], bounds[1:])
    ]
    size = own_rows // CORES
    if units == 4:
        sets = (((0, unit), (3 * unit, unit)), ((unit, 2 * unit),))
        halves = [jnp.concatenate([lots[0], lots[2]], axis=0), lots[1]]
    else:
        sets = tuple(((first, size),) for first in range(0, own_rows, size))
        left = jnp.concatenate(lots, axis=0) if len(lots) > 1 else lots[0]
        halves = [left[first : first + size] for first in range(0, own_rows, size)]

    def cross(rows, earlier):
        pair = []
        for dh in range(n_high):
            held = after(rows, *earlier[dh]) if earlier else rows
            pair.append(across(held, sizes, dh * CORES))
        return pair

    def relay(pair, earlier):
        if earlier:
            pair = [after(rows, *[sent[dh] for sent in earlier]) for dh, rows in enumerate(pair)]
        return pair, [[swap(rows, sizes, 0, 0, dk) for rows in pair] for dk in range(1, n_groups)]

    landed = cross(lots[0], [])
    both = []
    if units > 2:
        both = [lots[2]] + [swap(lots[2], sizes, 0, 0, dk) for dk in range(1, n_groups)]
    landed, others = relay(landed, [])
    pieces = [(landed, others, 0)]

    away = jnp.where(core == 0, halves[0], halves[1])
    widened = [swap(after(away, *landed), sizes, 0, dh * CORES, 0) for dh in range(1, n_high)]
    done = list(widened) + [rows for sent in others for rows in sent]

    crossed = landed
    if units > 1:
        crossed = cross(lots[1], [[rows] for rows in crossed])
        done += crossed
        landed, others = relay(crossed, others)
        pieces.append((landed, others, 1))
    if units > 2:
        landed = cross(jnp.concatenate(both, axis=0), [done] * n_high)
        pieces.append((landed, None, units - 1))

    rests = []
    for came in widened:
        came = after(came, *crossed)
        rests += [came, swap(came, sizes, 0, 1, 0)]
    turn = (row // CORES) ^ high
    wide = widen_left(sets, halves, rests, core, turn, own_rows)

    panel, columns = None, own_rows * n_groups

    def fill(pair, first, shifts):
        nonlocal panel
        count = pair[0].shape[0] // unit // len(shifts)
        places = [(group ^ dk) * units + first + at for dk in shifts for at in range(count)]
        panel = place_panel(wide, pair, unit, places, columns, panel)

    for pair, sent, first in pieces:
        if sent is not None:
            fill(pair, first, [0])
    for pair, sent, first in pieces[:1]:
        for dk in range(1, n_groups):
            fill(sent[dk - 1], first, [dk])
    for pair, sent, first in pieces[LAST:] + pieces[1:LAST]:
        if sent is None:
            fill(pair, first, list(range(n_groups)))
        else:
            for dk in range(1, n_groups):
                fill(sent[dk - 1], first, [dk])
    return panel


def solution(mesh):
    sizes = tuple(mesh.shape[axis] for axis in AXES)
    in_specs = (
        P(("prow", "pcol"), "pl"),
        P(None, ("prow", "pcol")),
        P(("prow", "pl"), None),
        P(),
        P(),
    )
    out_specs = P(("prow", "pl"), "pcol")
    return jax.shard_map(
        functools.partial(body, sizes), mesh=mesh, in_specs=in_specs, out_specs=out_specs, check_vma=False
    )
```

```python
import functools

import jax
import jax.numpy as jnp
from jax import lax
from jax.experimental import pallas as pl
from jax.experimental.pallas import tpu as pltpu
from jax.sharding import PartitionSpec as P

AXES = ("prow", "pcol", "pl")
CORES = 2
UNITS = 4
LANES = 128
LAST = 1
PROJECT = 48
MIB = 1024 * 1024


def transfer_pair(natural_freq, damping):
    detuning = natural_freq * natural_freq - 1.0
    damper = 2.0 * damping * natural_freq
    modulus = detuning * detuning + damper * damper
    return detuning / modulus, -damper / modulus


def moves(sizes, source_of):
    rows, cols, groups = sizes
    pairs = []
    for i in range(rows):
        for j in range(cols):
            for k in range(groups):
                a, b, c = source_of(i, j, k)
                pairs.append(((a * cols + b) * groups + c, (i * cols + j) * groups + k))
    return pairs


def swap(array, sizes, di, dj, dk):
    return lax.ppermute(array, AXES, moves(sizes, lambda i, j, k: (i ^ di, j ^ dj, k ^ dk)))


def across(array, sizes, flip):
    return lax.ppermute(array, AXES, moves(sizes, lambda i, j, k: (j, i ^ flip, k)))


def cheap():
    return pl.CostEstimate(flops=1, bytes_accessed=1, transcendentals=0)


def after(array, *earlier):
    return pl.pallas_call(
        lambda *refs: None,
        in_specs=[pl.BlockSpec(memory_space=pl.ANY)] * (1 + len(earlier)),
        out_specs=pl.BlockSpec(memory_space=pl.ANY),
        out_shape=jax.ShapeDtypeStruct(array.shape, array.dtype),
        input_output_aliases={0: 0},
        cost_estimate=cheap(),
    )(array, *earlier)


def outer_rows(left_rows, right_rows):
    return lax.dot_general(
        left_rows, right_rows, (((1,), (1,)), ((), ())), preferred_element_type=jnp.float32
    )


def gather_kernel(rows, wide, spots, *refs):
    out = refs[-1]
    count = len(refs) - 1
    parts = out.shape[0] // rows
    for at in range(count):
        dk, dr = divmod(at, parts)
        first = pl.multiple_of((spots[0] ^ dr) * rows, rows)
        left = pl.multiple_of((spots[1] ^ dk) * wide, wide)
        out[pl.ds(first, rows), pl.ds(left, wide)] = refs[at][...]


def gather_loads(blocks, row, group, parts):
    rows, wide = blocks[0].shape
    whole = pl.BlockSpec(memory_space=pltpu.VMEM)
    shape = (rows * parts, wide * (len(blocks) // parts))
    return pl.pallas_call(
        functools.partial(gather_kernel, rows, wide),
        in_specs=[pl.BlockSpec(memory_space=pltpu.SMEM)] + [whole] * len(blocks),
        out_specs=whole,
        out_shape=jax.ShapeDtypeStruct(shape, jnp.bfloat16),
        compiler_params=pltpu.CompilerParams(vmem_limit_bytes=8 * MIB),
        cost_estimate=cheap(),
    )(jnp.stack([row, group]).astype(jnp.int32), *blocks)


def project_kernel(spots, mine, theirs, scale, shapes, out, loads):
    half, wide = mine.shape

    @pl.when(pl.program_id(0) == 0)
    def _():
        strip = min(wide, LANES)
        for block, core in ((mine, spots[0]), (theirs, 1 - spots[0])):
            first = pl.multiple_of(core * half, half)

            @pl.loop(0, wide // strip)
            def _(at, block=block, first=first):
                left = pl.multiple_of(at * strip, strip)
                load = block[:, pl.ds(left, strip)].astype(jnp.float32)
                for part in range(2):
                    scaled = scale[part, pl.ds(first, half), :] * load
                    place = pl.multiple_of(part * wide + at * strip, strip)
                    loads[pl.ds(first, half), pl.ds(place, strip)] = scaled.astype(loads.dtype)

    out[...] = jnp.dot(shapes[...], loads[...], preferred_element_type=jnp.float32).astype(out.dtype)


def project(shapes, mine, theirs, scale, core, span, tile, limit):
    modes, wide = shapes.shape[1], 2 * mine.shape[1]
    first, rows = span[0], (span[1] - span[0]) * tile
    whole = pl.BlockSpec(memory_space=pltpu.VMEM)
    return pl.pallas_call(
        project_kernel,
        grid_spec=pltpu.PrefetchScalarGridSpec(
            num_scalar_prefetch=1,
            grid=(rows // tile,),
            in_specs=[whole] * 3 + [pl.BlockSpec((tile, modes), lambda g, spots: (first + g, 0))],
            out_specs=pl.BlockSpec((tile, wide), lambda g, spots: (g, 0)),
            scratch_shapes=[pltpu.VMEM((modes, wide), jnp.bfloat16)],
        ),
        out_shape=jax.ShapeDtypeStruct((rows, wide), jnp.bfloat16),
        compiler_params=pltpu.CompilerParams(vmem_limit_bytes=(limit if wide <= modes else PROJECT) * MIB),
        cost_estimate=cheap(),
    )(jnp.reshape(core, (1,)).astype(jnp.int32), mine, theirs, scale, shapes)


def widen_kernel(sets, spots, *refs):
    out, own, refs = refs[-1], refs[: len(sets)], refs[len(sets) : -1]
    deep = own[0].shape[1]

    def lay(array, spans, place):
        left, low = pl.multiple_of(place * deep, deep), 0
        for first, count in spans:
            out[first : first + count, pl.ds(left, deep)] = array[low : low + count, :]
            low += count

    for at, spans in enumerate(sets):
        lay(own[at], spans, spots[1])
    for core in range(len(sets)):

        @pl.when(spots[0] == core)
        def _(core=core):
            for at in range(0, len(refs), len(sets)):
                place = spots[1] ^ (at // len(sets) + 1)
                for d in range(len(sets)):
                    lay(refs[at + d], sets[core ^ d], place)


def widen_left(sets, own, others, core, turn, rows):
    whole = pl.BlockSpec(memory_space=pltpu.VMEM)
    deep = own[0].shape[1]
    wide = deep * (1 + len(others) // len(sets))
    return pl.pallas_call(
        functools.partial(widen_kernel, sets),
        in_specs=[pl.BlockSpec(memory_space=pltpu.SMEM)] + [whole] * (len(own) + len(others)),
        out_specs=whole,
        out_shape=jax.ShapeDtypeStruct((rows, wide), jnp.bfloat16),
        compiler_params=pltpu.CompilerParams(vmem_limit_bytes=8 * MIB),
        cost_estimate=cheap(),
    )(jnp.stack([core, turn]).astype(jnp.int32), *own, *others)


def panel_kernel(chunk, count, spots, left, *refs):
    first = pl.multiple_of(pl.program_id(0) * chunk, chunk)
    right = jnp.concatenate([piece[pl.ds(first, chunk), :] for piece in refs[:count]], axis=1)
    refs[-1][...] = outer_rows(left[...], right)


def place_panel(left, pieces, chunk, places, columns, panel):
    rows = left.shape[0]
    given = [] if panel is None else [panel]
    whole = pl.BlockSpec(memory_space=pltpu.VMEM)
    return pl.pallas_call(
        functools.partial(panel_kernel, chunk, len(pieces)),
        grid_spec=pltpu.PrefetchScalarGridSpec(
            num_scalar_prefetch=1,
            grid=(len(places),),
            in_specs=[whole] * (1 + len(pieces)) + [pl.BlockSpec(memory_space=pl.ANY) for _ in given],
            out_specs=pl.BlockSpec((rows, chunk), lambda g, spots: (0, spots[g])),
        ),
        out_shape=jax.ShapeDtypeStruct((rows, columns), jnp.float32),
        input_output_aliases={2 + len(pieces): 0} if given else {},
        compiler_params=pltpu.CompilerParams(vmem_limit_bytes=8 * MIB),
        cost_estimate=cheap(),
    )(jnp.stack(places).astype(jnp.int32), left, *pieces, *given)


def body(sizes, factor_cols, modal_at_loads, mode_shapes, natural_freq, damping):
    n_rows, n_cols, n_groups = sizes
    n_high = n_cols // CORES
    row, col, group = (lax.axis_index(axis) for axis in AXES)
    high, core = col // CORES, col % CORES
    scale = jnp.stack(transfer_pair(natural_freq, damping))[:, :, None]
    scale = jnp.broadcast_to(scale, scale.shape[:2] + (LANES,))
    own_rows, modes = mode_shapes.shape

    part = factor_cols.shape[1] // n_high
    block = modes // CORES // n_rows
    half = block * n_rows
    near = n_rows // 2
    size = half // 2

    def partial(which, side):
        rows = lax.dynamic_slice_in_dim(modal_at_loads, which * half + side * size, size, 0)
        return jnp.dot(rows, factor_cols, preferred_element_type=jnp.float32)

    own = None
    for part_of, side in ((1, (row // near) ^ 1), (0, row // near)):
        came = swap(partial(1 - core, side).astype(jnp.bfloat16), sizes, 0, 1, 0)
        total = (partial(core, side) + came.astype(jnp.float32)).astype(jnp.bfloat16)
        for dh in range(n_high):
            for dr in range(near):
                first = ((row ^ dr) % near) * block
                piece = lax.dynamic_slice(total, (first, (high ^ dh) * part), (block, part))
                if dh or dr or part_of:
                    piece = swap(piece, sizes, dr + part_of * near, dh * CORES, 0)
                piece = piece.astype(jnp.float32)
                own = piece if own is None else own + piece
    own = own.astype(jnp.bfloat16)
    line = [swap(own, sizes, dr, 0, 0) if dr else own for dr in range(n_rows)]
    blocks = list(line)
    for dk in range(1, n_groups):
        blocks += [swap(piece, sizes, 0, 0, dk) for piece in line]
    mine = gather_loads(blocks, row, group, n_rows)
    theirs = swap(mine, sizes, 0, 1, 0)

    unit = max(own_rows // UNITS, min(own_rows, 128))
    units = own_rows // unit
    bounds = (0, 1, units - 1, units) if units > 2 else tuple(range(units + 1))
    lots = [project(mode_shapes[: bounds[1] * unit], mine, theirs, scale, core, (0, bounds[1]), unit, 14)]
    for first, last in zip(bounds[1:-1], bounds[2:]):
        lots.append(project(mode_shapes, mine, theirs, scale, core, (first, last), unit, 14))
    size = own_rows // CORES
    if units == 4:
        sets = (((0, unit), (3 * unit, unit)), ((unit, 2 * unit),))
        halves = [jnp.concatenate([lots[0], lots[2]], axis=0), lots[1]]
    else:
        sets = tuple(((first, size),) for first in range(0, own_rows, size))
        left = jnp.concatenate(lots, axis=0) if len(lots) > 1 else lots[0]
        halves = [left[first : first + size] for first in range(0, own_rows, size)]

    def cross(rows, earlier):
        pair = []
        for dh in range(n_high):
            held = after(rows, *earlier[dh]) if earlier else rows
            pair.append(across(held, sizes, dh * CORES))
        return pair

    def relay(pair, earlier):
        if earlier:
            pair = [after(rows, *[sent[dh] for sent in earlier]) for dh, rows in enumerate(pair)]
        return pair, [[swap(rows, sizes, 0, 0, dk) for rows in pair] for dk in range(1, n_groups)]

    landed = cross(lots[0], [])
    both = []
    if units > 2:
        both = [lots[2]] + [swap(lots[2], sizes, 0, 0, dk) for dk in range(1, n_groups)]
    landed, others = relay(landed, [])
    pieces = [(landed, others, 0)]

    away = jnp.where(core == 0, halves[0], halves[1])
    widened = [swap(after(away, *landed), sizes, 0, dh * CORES, 0) for dh in range(1, n_high)]
    done = list(widened) + [rows for sent in others for rows in sent]

    crossed = landed
    if units > 1:
        crossed = cross(lots[1], [[rows] for rows in crossed])
        done += crossed
        landed, others = relay(crossed, others)
        pieces.append((landed, others, 1))
    if units > 2:
        landed = cross(jnp.concatenate(both, axis=0), [done] * n_high)
        pieces.append((landed, None, units - 1))

    rests = []
    for came in widened:
        came = after(came, *crossed)
        rests += [came, swap(came, sizes, 0, 1, 0)]
    turn = (row // CORES) ^ high
    wide = widen_left(sets, halves, rests, core, turn, own_rows)

    panel, columns = None, own_rows * n_groups

    def fill(pair, first, shifts):
        nonlocal panel
        count = pair[0].shape[0] // unit // len(shifts)
        places = [(group ^ dk) * units + first + at for dk in shifts for at in range(count)]
        panel = place_panel(wide, pair, unit, places, columns, panel)

    for pair, sent, first in pieces:
        if sent is not None:
            fill(pair, first, [0])
    for pair, sent, first in pieces[:1]:
        for dk in range(1, n_groups):
            fill(sent[dk - 1], first, [dk])
    for pair, sent, first in pieces[LAST:] + pieces[1:LAST]:
        if sent is None:
            fill(pair, first, list(range(n_groups)))
        else:
            for dk in range(1, n_groups):
                fill(sent[dk - 1], first, [dk])
    return panel


def solution(mesh):
    sizes = tuple(mesh.shape[axis] for axis in AXES)
    in_specs = (
        P(("prow", "pcol"), "pl"),
        P(None, ("prow", "pcol")),
        P(("prow", "pl"), None),
        P(),
        P(),
    )
    out_specs = P(("prow", "pl"), "pcol")
    return jax.shard_map(
        functools.partial(body, sizes), mesh=mesh, in_specs=in_specs, out_specs=out_specs, check_vma=False
    )
```

```python
import functools

import jax
import jax.numpy as jnp
from jax import lax
from jax.experimental import pallas as pl
from jax.experimental.pallas import tpu as pltpu
from jax.sharding import PartitionSpec as P

AXES = ("prow", "pcol", "pl")
CORES = 2
UNITS = 4
LANES = 128
LAST = 1
PROJECT = 48
MIB = 1024 * 1024


def transfer_pair(natural_freq, damping):
    detuning = natural_freq * natural_freq - 1.0
    damper = 2.0 * damping * natural_freq
    modulus = detuning * detuning + damper * damper
    return detuning / modulus, -damper / modulus


def moves(sizes, source_of):
    rows, cols, groups = sizes
    pairs = []
    for i in range(rows):
        for j in range(cols):
            for k in range(groups):
                a, b, c = source_of(i, j, k)
                pairs.append(((a * cols + b) * groups + c, (i * cols + j) * groups + k))
    return pairs


def swap(array, sizes, di, dj, dk):
    return lax.ppermute(array, AXES, moves(sizes, lambda i, j, k: (i ^ di, j ^ dj, k ^ dk)))


def across(array, sizes, flip):
    return lax.ppermute(array, AXES, moves(sizes, lambda i, j, k: (j, i ^ flip, k)))


def cheap():
    return pl.CostEstimate(flops=1, bytes_accessed=1, transcendentals=0)


def after(array, *earlier):
    return pl.pallas_call(
        lambda *refs: None,
        in_specs=[pl.BlockSpec(memory_space=pl.ANY)] * (1 + len(earlier)),
        out_specs=pl.BlockSpec(memory_space=pl.ANY),
        out_shape=jax.ShapeDtypeStruct(array.shape, array.dtype),
        input_output_aliases={0: 0},
        cost_estimate=cheap(),
    )(array, *earlier)


def outer_rows(left_rows, right_rows):
    return lax.dot_general(
        left_rows, right_rows, (((1,), (1,)), ((), ())), preferred_element_type=jnp.float32
    )


def gather_kernel(rows, wide, spots, *refs):
    out = refs[-1]
    count = len(refs) - 1
    parts = out.shape[0] // rows
    for at in range(count):
        dk, dr = divmod(at, parts)
        first = pl.multiple_of((spots[0] ^ dr) * rows, rows)
        left = pl.multiple_of((spots[1] ^ dk) * wide, wide)
        out[pl.ds(first, rows), pl.ds(left, wide)] = refs[at][...]


def gather_loads(blocks, row, group, parts):
    rows, wide = blocks[0].shape
    whole = pl.BlockSpec(memory_space=pltpu.VMEM)
    shape = (rows * parts, wide * (len(blocks) // parts))
    return pl.pallas_call(
        functools.partial(gather_kernel, rows, wide),
        in_specs=[pl.BlockSpec(memory_space=pltpu.SMEM)] + [whole] * len(blocks),
        out_specs=whole,
        out_shape=jax.ShapeDtypeStruct(shape, jnp.bfloat16),
        compiler_params=pltpu.CompilerParams(vmem_limit_bytes=8 * MIB),
        cost_estimate=cheap(),
    )(jnp.stack([row, group]).astype(jnp.int32), *blocks)


def project_kernel(spots, mine, theirs, scale, shapes, out, loads):
    half, wide = mine.shape

    @pl.when(pl.program_id(0) == 0)
    def _():
        strip = min(wide, LANES)
        for block, core in ((mine, spots[0]), (theirs, 1 - spots[0])):
            first = pl.multiple_of(core * half, half)

            @pl.loop(0, wide // strip)
            def _(at, block=block, first=first):
                left = pl.multiple_of(at * strip, strip)
                load = block[:, pl.ds(left, strip)].astype(jnp.float32)
                for part in range(2):
                    scaled = scale[part, pl.ds(first, half), :] * load
                    place = pl.multiple_of(part * wide + at * strip, strip)
                    loads[pl.ds(first, half), pl.ds(place, strip)] = scaled.astype(loads.dtype)

    out[...] = jnp.dot(shapes[...], loads[...], preferred_element_type=jnp.float32).astype(out.dtype)


def project(shapes, mine, theirs, scale, core, span, tile, limit):
    modes, wide = shapes.shape[1], 2 * mine.shape[1]
    first, rows = span[0], (span[1] - span[0]) * tile
    whole = pl.BlockSpec(memory_space=pltpu.VMEM)
    return pl.pallas_call(
        project_kernel,
        grid_spec=pltpu.PrefetchScalarGridSpec(
            num_scalar_prefetch=1,
            grid=(rows // tile,),
            in_specs=[whole] * 3 + [pl.BlockSpec((tile, modes), lambda g, spots: (first + g, 0))],
            out_specs=pl.BlockSpec((tile, wide), lambda g, spots: (g, 0)),
            scratch_shapes=[pltpu.VMEM((modes, wide), jnp.bfloat16)],
        ),
        out_shape=jax.ShapeDtypeStruct((rows, wide), jnp.bfloat16),
        compiler_params=pltpu.CompilerParams(vmem_limit_bytes=(limit if wide <= modes else PROJECT) * MIB),
        cost_estimate=cheap(),
    )(jnp.reshape(core, (1,)).astype(jnp.int32), mine, theirs, scale, shapes)


def widen_kernel(sets, spots, *refs):
    out, own, refs = refs[-1], refs[: len(sets)], refs[len(sets) : -1]
    deep = own[0].shape[1]

    def lay(array, spans, place):
        left, low = pl.multiple_of(place * deep, deep), 0
        for first, count in spans:
            out[first : first + count, pl.ds(left, deep)] = array[low : low + count, :]
            low += count

    for at, spans in enumerate(sets):
        lay(own[at], spans, spots[1])
    for core in range(len(sets)):

        @pl.when(spots[0] == core)
        def _(core=core):
            for at in range(0, len(refs), len(sets)):
                place = spots[1] ^ (at // len(sets) + 1)
                for d in range(len(sets)):
                    lay(refs[at + d], sets[core ^ d], place)


def widen_left(sets, own, others, core, turn, rows):
    whole = pl.BlockSpec(memory_space=pltpu.VMEM)
    deep = own[0].shape[1]
    wide = deep * (1 + len(others) // len(sets))
    return pl.pallas_call(
        functools.partial(widen_kernel, sets),
        in_specs=[pl.BlockSpec(memory_space=pltpu.SMEM)] + [whole] * (len(own) + len(others)),
        out_specs=whole,
        out_shape=jax.ShapeDtypeStruct((rows, wide), jnp.bfloat16),
        compiler_params=pltpu.CompilerParams(vmem_limit_bytes=8 * MIB),
        cost_estimate=cheap(),
    )(jnp.stack([core, turn]).astype(jnp.int32), *own, *others)


def panel_kernel(count, spots, left, *refs):
    right = jnp.concatenate([piece[...] for piece in refs[:count]], axis=1)
    refs[-1][...] = outer_rows(left[...], right)


def place_panel(left, pieces, chunk, places, columns, panel):
    rows = left.shape[0]
    given = [] if panel is None else [panel]
    whole = pl.BlockSpec(memory_space=pltpu.VMEM)
    return pl.pallas_call(
        functools.partial(panel_kernel, len(pieces)),
        grid_spec=pltpu.PrefetchScalarGridSpec(
            num_scalar_prefetch=1,
            grid=(len(places),),
            in_specs=[whole]
            + [pl.BlockSpec((chunk, piece.shape[1]), lambda g, spots: (g, 0)) for piece in pieces]
            + [pl.BlockSpec(memory_space=pl.ANY) for _ in given],
            out_specs=pl.BlockSpec((rows, chunk), lambda g, spots: (0, spots[g])),
        ),
        out_shape=jax.ShapeDtypeStruct((rows, columns), jnp.float32),
        input_output_aliases={2 + len(pieces): 0} if given else {},
        compiler_params=pltpu.CompilerParams(vmem_limit_bytes=8 * MIB),
        cost_estimate=cheap(),
    )(jnp.stack(places).astype(jnp.int32), left, *pieces, *given)


def body(sizes, factor_cols, modal_at_loads, mode_shapes, natural_freq, damping):
    n_rows, n_cols, n_groups = sizes
    n_high = n_cols // CORES
    row, col, group = (lax.axis_index(axis) for axis in AXES)
    high, core = col // CORES, col % CORES
    scale = jnp.stack(transfer_pair(natural_freq, damping))[:, :, None]
    scale = jnp.broadcast_to(scale, scale.shape[:2] + (LANES,))
    own_rows, modes = mode_shapes.shape

    part = factor_cols.shape[1] // n_high
    block = modes // CORES // n_rows
    half = block * n_rows
    near = n_rows // 2
    size = half // 2

    def partial(which, side):
        rows = lax.dynamic_slice_in_dim(modal_at_loads, which * half + side * size, size, 0)
        return jnp.dot(rows, factor_cols, preferred_element_type=jnp.float32)

    own = None
    for part_of, side in ((1, (row // near) ^ 1), (0, row // near)):
        came = swap(partial(1 - core, side).astype(jnp.bfloat16), sizes, 0, 1, 0)
        total = (partial(core, side) + came.astype(jnp.float32)).astype(jnp.bfloat16)
        for dh in range(n_high):
            for dr in range(near):
                first = ((row ^ dr) % near) * block
                piece = lax.dynamic_slice(total, (first, (high ^ dh) * part), (block, part))
                if dh or dr or part_of:
                    piece = swap(piece, sizes, dr + part_of * near, dh * CORES, 0)
                piece = piece.astype(jnp.float32)
                own = piece if own is None else own + piece
    own = own.astype(jnp.bfloat16)
    line = [swap(own, sizes, dr, 0, 0) if dr else own for dr in range(n_rows)]
    blocks = list(line)
    for dk in range(1, n_groups):
        blocks += [swap(piece, sizes, 0, 0, dk) for piece in line]
    mine = gather_loads(blocks, row, group, n_rows)
    theirs = swap(mine, sizes, 0, 1, 0)

    unit = max(own_rows // UNITS, min(own_rows, 128))
    units = own_rows // unit
    bounds = (0, 1, units - 1, units) if units > 2 else tuple(range(units + 1))
    lots = [project(mode_shapes[: bounds[1] * unit], mine, theirs, scale, core, (0, bounds[1]), unit, 14)]
    for first, last in zip(bounds[1:-1], bounds[2:]):
        lots.append(project(mode_shapes, mine, theirs, scale, core, (first, last), unit, 14))
    size = own_rows // CORES
    if units == 4:
        sets = (((0, unit), (3 * unit, unit)), ((unit, 2 * unit),))
        halves = [jnp.concatenate([lots[0], lots[2]], axis=0), lots[1]]
    else:
        sets = tuple(((first, size),) for first in range(0, own_rows, size))
        left = jnp.concatenate(lots, axis=0) if len(lots) > 1 else lots[0]
        halves = [left[first : first + size] for first in range(0, own_rows, size)]

    def cross(rows, earlier):
        pair = []
        for dh in range(n_high):
            held = after(rows, *earlier[dh]) if earlier else rows
            pair.append(across(held, sizes, dh * CORES))
        return pair

    def relay(pair, earlier):
        if earlier:
            pair = [after(rows, *[sent[dh] for sent in earlier]) for dh, rows in enumerate(pair)]
        return pair, [[swap(rows, sizes, 0, 0, dk) for rows in pair] for dk in range(1, n_groups)]

    landed = cross(lots[0], [])
    both = []
    if units > 2:
        both = [lots[2]] + [swap(lots[2], sizes, 0, 0, dk) for dk in range(1, n_groups)]
    landed, others = relay(landed, [])
    pieces = [(landed, others, 0)]

    away = jnp.where(core == 0, halves[0], halves[1])
    widened = [swap(after(away, *landed), sizes, 0, dh * CORES, 0) for dh in range(1, n_high)]
    done = list(widened) + [rows for sent in others for rows in sent]

    crossed = landed
    if units > 1:
        crossed = cross(lots[1], [[rows] for rows in crossed])
        done += crossed
        landed, others = relay(crossed, others)
        pieces.append((landed, others, 1))
    if units > 2:
        landed = cross(jnp.concatenate(both, axis=0), [done] * n_high)
        pieces.append((landed, None, units - 1))

    rests = []
    for came in widened:
        came = after(came, *crossed)
        rests += [came, swap(came, sizes, 0, 1, 0)]
    turn = (row // CORES) ^ high
    wide = widen_left(sets, halves, rests, core, turn, own_rows)

    panel, columns = None, own_rows * n_groups

    def fill(pair, first, shifts):
        nonlocal panel
        count = pair[0].shape[0] // unit // len(shifts)
        places = [(group ^ dk) * units + first + at for dk in shifts for at in range(count)]
        panel = place_panel(wide, pair, unit, places, columns, panel)

    for pair, sent, first in pieces:
        if sent is not None:
            fill(pair, first, [0])
    for pair, sent, first in pieces[:1]:
        for dk in range(1, n_groups):
            fill(sent[dk - 1], first, [dk])
    for pair, sent, first in pieces[LAST:] + pieces[1:LAST]:
        if sent is None:
            fill(pair, first, list(range(n_groups)))
        else:
            for dk in range(1, n_groups):
                fill(sent[dk - 1], first, [dk])
    return panel


def solution(mesh):
    sizes = tuple(mesh.shape[axis] for axis in AXES)
    in_specs = (
        P(("prow", "pcol"), "pl"),
        P(None, ("prow", "pcol")),
        P(("prow", "pl"), None),
        P(),
        P(),
    )
    out_specs = P(("prow", "pl"), "pcol")
    return jax.shard_map(
        functools.partial(body, sizes), mesh=mesh, in_specs=in_specs, out_specs=out_specs, check_vma=False
    )
```

```python
import functools

import jax
import jax.numpy as jnp
from jax import lax
from jax.experimental import pallas as pl
from jax.experimental.pallas import tpu as pltpu
from jax.sharding import PartitionSpec as P

AXES = ("prow", "pcol", "pl")
CORES = 2
UNITS = 4
LANES = 128
LAST = 1
PROJECT = 48
MIB = 1024 * 1024


def transfer_pair(natural_freq, damping):
    detuning = natural_freq * natural_freq - 1.0
    damper = 2.0 * damping * natural_freq
    modulus = detuning * detuning + damper * damper
    return detuning / modulus, -damper / modulus


def moves(sizes, source_of):
    rows, cols, groups = sizes
    pairs = []
    for i in range(rows):
        for j in range(cols):
            for k in range(groups):
                a, b, c = source_of(i, j, k)
                pairs.append(((a * cols + b) * groups + c, (i * cols + j) * groups + k))
    return pairs


def swap(array, sizes, di, dj, dk):
    return lax.ppermute(array, AXES, moves(sizes, lambda i, j, k: (i ^ di, j ^ dj, k ^ dk)))


def across(array, sizes, flip):
    return lax.ppermute(array, AXES, moves(sizes, lambda i, j, k: (j, i ^ flip, k)))


def cheap():
    return pl.CostEstimate(flops=1, bytes_accessed=1, transcendentals=0)


def after(array, *earlier):
    return pl.pallas_call(
        lambda *refs: None,
        in_specs=[pl.BlockSpec(memory_space=pl.ANY)] * (1 + len(earlier)),
        out_specs=pl.BlockSpec(memory_space=pl.ANY),
        out_shape=jax.ShapeDtypeStruct(array.shape, array.dtype),
        input_output_aliases={0: 0},
        cost_estimate=cheap(),
    )(array, *earlier)


def outer_rows(left_rows, right_rows):
    return lax.dot_general(
        left_rows, right_rows, (((1,), (1,)), ((), ())), preferred_element_type=jnp.float32
    )


def gather_kernel(rows, wide, spots, *refs):
    out = refs[-1]
    count = len(refs) - 1
    parts = out.shape[0] // rows
    for at in range(count):
        dk, dr = divmod(at, parts)
        first = pl.multiple_of((spots[0] ^ dr) * rows, rows)
        left = pl.multiple_of((spots[1] ^ dk) * wide, wide)
        out[pl.ds(first, rows), pl.ds(left, wide)] = refs[at][...]


def gather_loads(blocks, row, group, parts):
    rows, wide = blocks[0].shape
    whole = pl.BlockSpec(memory_space=pltpu.VMEM)
    shape = (rows * parts, wide * (len(blocks) // parts))
    return pl.pallas_call(
        functools.partial(gather_kernel, rows, wide),
        in_specs=[pl.BlockSpec(memory_space=pltpu.SMEM)] + [whole] * len(blocks),
        out_specs=whole,
        out_shape=jax.ShapeDtypeStruct(shape, jnp.bfloat16),
        compiler_params=pltpu.CompilerParams(vmem_limit_bytes=8 * MIB),
        cost_estimate=cheap(),
    )(jnp.stack([row, group]).astype(jnp.int32), *blocks)


def project_kernel(spots, mine, theirs, scale, shapes, out, loads):
    half, wide = mine.shape

    @pl.when(pl.program_id(0) == 0)
    def _():
        strip = min(wide, LANES)
        for block, core in ((mine, spots[0]), (theirs, 1 - spots[0])):
            first = pl.multiple_of(core * half, half)

            @pl.loop(0, wide // strip)
            def _(at, block=block, first=first):
                left = pl.multiple_of(at * strip, strip)
                load = block[:, pl.ds(left, strip)].astype(jnp.float32)
                for part in range(2):
                    scaled = scale[part, pl.ds(first, half), :] * load
                    place = pl.multiple_of(part * wide + at * strip, strip)
                    loads[pl.ds(first, half), pl.ds(place, strip)] = scaled.astype(loads.dtype)

    out[...] = jnp.dot(shapes[...], loads[...], preferred_element_type=jnp.float32).astype(out.dtype)


def project(shapes, mine, theirs, scale, core, span, tile, limit):
    modes, wide = shapes.shape[1], 2 * mine.shape[1]
    first, rows = span[0], (span[1] - span[0]) * tile
    whole = pl.BlockSpec(memory_space=pltpu.VMEM)
    return pl.pallas_call(
        project_kernel,
        grid_spec=pltpu.PrefetchScalarGridSpec(
            num_scalar_prefetch=1,
            grid=(rows // tile,),
            in_specs=[whole] * 3 + [pl.BlockSpec((tile, modes), lambda g, spots: (first + g, 0))],
            out_specs=pl.BlockSpec((tile, wide), lambda g, spots: (g, 0)),
            scratch_shapes=[pltpu.VMEM((modes, wide), jnp.bfloat16)],
        ),
        out_shape=jax.ShapeDtypeStruct((rows, wide), jnp.bfloat16),
        compiler_params=pltpu.CompilerParams(vmem_limit_bytes=(limit if wide <= modes else PROJECT) * MIB),
        cost_estimate=cheap(),
    )(jnp.reshape(core, (1,)).astype(jnp.int32), mine, theirs, scale, shapes)


def widen_kernel(sets, spots, *refs):
    out, own, refs = refs[-1], refs[: len(sets)], refs[len(sets) : -1]
    deep = own[0].shape[1]

    def lay(array, spans, place):
        left, low = pl.multiple_of(place * deep, deep), 0
        for first, count in spans:
            out[first : first + count, pl.ds(left, deep)] = array[low : low + count, :]
            low += count

    for at, spans in enumerate(sets):
        lay(own[at], spans, spots[1])
    for core in range(len(sets)):

        @pl.when(spots[0] == core)
        def _(core=core):
            for at in range(0, len(refs), len(sets)):
                place = spots[1] ^ (at // len(sets) + 1)
                for d in range(len(sets)):
                    lay(refs[at + d], sets[core ^ d], place)


def widen_left(sets, own, others, core, turn, rows):
    whole = pl.BlockSpec(memory_space=pltpu.VMEM)
    deep = own[0].shape[1]
    wide = deep * (1 + len(others) // len(sets))
    return pl.pallas_call(
        functools.partial(widen_kernel, sets),
        in_specs=[pl.BlockSpec(memory_space=pltpu.SMEM)] + [whole] * (len(own) + len(others)),
        out_specs=whole,
        out_shape=jax.ShapeDtypeStruct((rows, wide), jnp.bfloat16),
        compiler_params=pltpu.CompilerParams(vmem_limit_bytes=8 * MIB),
        cost_estimate=cheap(),
    )(jnp.stack([core, turn]).astype(jnp.int32), *own, *others)


def panel_kernel(count, spots, left, *refs):
    right = jnp.concatenate([piece[...] for piece in refs[:count]], axis=1)
    refs[-1][...] = outer_rows(left[...], right)


def place_panel(left, pieces, chunk, places, columns, panel):
    rows = left.shape[0]
    given = [] if panel is None else [panel]
    whole = pl.BlockSpec(memory_space=pltpu.VMEM)
    return pl.pallas_call(
        functools.partial(panel_kernel, len(pieces)),
        grid_spec=pltpu.PrefetchScalarGridSpec(
            num_scalar_prefetch=1,
            grid=(len(places),),
            in_specs=[whole]
            + [pl.BlockSpec((chunk, piece.shape[1]), lambda g, spots: (g, 0)) for piece in pieces]
            + [pl.BlockSpec(memory_space=pl.ANY) for _ in given],
            out_specs=pl.BlockSpec((rows, chunk), lambda g, spots: (0, spots[g])),
        ),
        out_shape=jax.ShapeDtypeStruct((rows, columns), jnp.float32),
        input_output_aliases={2 + len(pieces): 0} if given else {},
        compiler_params=pltpu.CompilerParams(vmem_limit_bytes=8 * MIB),
        cost_estimate=cheap(),
    )(jnp.stack(places).astype(jnp.int32), left, *pieces, *given)


def body(sizes, factor_cols, modal_at_loads, mode_shapes, natural_freq, damping):
    n_rows, n_cols, n_groups = sizes
    n_high = n_cols // CORES
    row, col, group = (lax.axis_index(axis) for axis in AXES)
    high, core = col // CORES, col % CORES
    scale = jnp.stack(transfer_pair(natural_freq, damping))[:, :, None]
    scale = jnp.broadcast_to(scale, scale.shape[:2] + (LANES,))
    own_rows, modes = mode_shapes.shape

    part = factor_cols.shape[1] // n_high
    block = modes // CORES // n_rows
    half = block * n_rows
    near = n_rows // 2
    size = half // 2

    def partial(which, side):
        rows = lax.dynamic_slice_in_dim(modal_at_loads, which * half + side * size, size, 0)
        return jnp.dot(rows, factor_cols, preferred_element_type=jnp.float32)

    own = None
    for part_of, side in ((1, (row // near) ^ 1), (0, row // near)):
        came = swap(partial(1 - core, side).astype(jnp.bfloat16), sizes, 0, 1, 0)
        total = (partial(core, side) + came.astype(jnp.float32)).astype(jnp.bfloat16)
        for dh in range(n_high):
            for dr in range(near):
                first = ((row ^ dr) % near) * block
                piece = lax.dynamic_slice(total, (first, (high ^ dh) * part), (block, part))
                if dh or dr or part_of:
                    piece = swap(piece, sizes, dr + part_of * near, dh * CORES, 0)
                piece = piece.astype(jnp.float32)
                own = piece if own is None else own + piece
    own = own.astype(jnp.bfloat16)
    line = [swap(own, sizes, dr, 0, 0) if dr else own for dr in range(n_rows)]
    blocks = list(line)
    for dk in range(1, n_groups):
        blocks += [swap(piece, sizes, 0, 0, dk) for piece in line]
    mine = gather_loads(blocks, row, group, n_rows)
    theirs = swap(mine, sizes, 0, 1, 0)

    unit = max(own_rows // UNITS, min(own_rows, 128))
    units = own_rows // unit
    bounds = (0, 1, units - 1, units) if units > 2 else tuple(range(units + 1))
    lots = [project(mode_shapes[: bounds[1] * unit], mine, theirs, scale, core, (0, bounds[1]), unit, 14)]
    for first, last in zip(bounds[1:-1], bounds[2:]):
        lots.append(project(mode_shapes, mine, theirs, scale, core, (first, last), unit, 14))
    size = own_rows // CORES
    if units == 4:
        sets = (((0, unit), (3 * unit, unit)), ((unit, 2 * unit),))
        halves = [jnp.concatenate([lots[0], lots[2]], axis=0), lots[1]]
    else:
        sets = tuple(((first, size),) for first in range(0, own_rows, size))
        left = jnp.concatenate(lots, axis=0) if len(lots) > 1 else lots[0]
        halves = [left[first : first + size] for first in range(0, own_rows, size)]

    def cross(rows, earlier):
        pair = []
        for dh in range(n_high):
            held = after(rows, *earlier[dh]) if earlier else rows
            pair.append(across(held, sizes, dh * CORES))
        return pair

    def relay(pair, earlier):
        if earlier:
            pair = [after(rows, *[sent[dh] for sent in earlier]) for dh, rows in enumerate(pair)]
        return pair, [[swap(rows, sizes, 0, 0, dk) for rows in pair] for dk in range(1, n_groups)]

    landed = cross(lots[0], [])
    both = []
    if units > 2:
        held = after(lots[2], landed[0])
        both = [held] + [swap(held, sizes, 0, 0, dk) for dk in range(1, n_groups)]
    landed, others = relay(landed, [])
    pieces = [(landed, others, 0)]

    away = jnp.where(core == 0, halves[0], halves[1])
    widened = [swap(after(away, *landed), sizes, 0, dh * CORES, 0) for dh in range(1, n_high)]
    done = list(widened) + [rows for sent in others for rows in sent]

    crossed = landed
    if units > 1:
        crossed = cross(lots[1], [[rows] for rows in crossed])
        done += crossed
        landed, others = relay(crossed, others)
        pieces.append((landed, others, 1))
    if units > 2:
        landed = cross(jnp.concatenate(both, axis=0), [done] * n_high)
        pieces.append((landed, None, units - 1))

    rests = []
    for came in widened:
        came = after(came, *crossed)
        rests += [came, swap(came, sizes, 0, 1, 0)]
    turn = (row // CORES) ^ high
    wide = widen_left(sets, halves, rests, core, turn, own_rows)

    panel, columns = None, own_rows * n_groups

    def fill(pair, first, shifts):
        nonlocal panel
        count = pair[0].shape[0] // unit // len(shifts)
        places = [(group ^ dk) * units + first + at for dk in shifts for at in range(count)]
        panel = place_panel(wide, pair, unit, places, columns, panel)

    for pair, sent, first in pieces:
        if sent is not None:
            fill(pair, first, [0])
    for pair, sent, first in pieces[:1]:
        for dk in range(1, n_groups):
            fill(sent[dk - 1], first, [dk])
    for pair, sent, first in pieces[LAST:] + pieces[1:LAST]:
        if sent is None:
            fill(pair, first, list(range(n_groups)))
        else:
            for dk in range(1, n_groups):
                fill(sent[dk - 1], first, [dk])
    return panel


def solution(mesh):
    sizes = tuple(mesh.shape[axis] for axis in AXES)
    in_specs = (
        P(("prow", "pcol"), "pl"),
        P(None, ("prow", "pcol")),
        P(("prow", "pl"), None),
        P(),
        P(),
    )
    out_specs = P(("prow", "pl"), "pcol")
    return jax.shard_map(
        functools.partial(body, sizes), mesh=mesh, in_specs=in_specs, out_specs=out_specs, check_vma=False
    )
```
